32 devices in a mesh: space: 4 (over z), chaos: 8 (over y, x, core).
Axes of the slice: x: 2, y: 2, z: 4, core: 2. Of those that a mesh axis runs over, the one named last changes fastest.
Arguments:
- forcing: float32 [912, 16, 128], P('chaos', 'space'), may hold values from -120 to 120
- mean_field: float32 [16, 128], P('space'), may hold values from 1 to 8
- modes: float32 [12, 16, 128], P(None, 'space'), may hold values from 0.02 to 0.05
- lengths: int32 [8], replicated, may hold values from 1 to 114, 455 in all
Outputs:
- solution: float32 [912, 16, 128], P('chaos', 'space')
- norms: float32 [3], replicated
The draws below stay inside these ranges and needn't reach their ends.
Inputs may be any that keep to these rules, and one draw needn't show every extreme that they name: Group lengths are positive, sum to 455, and the largest is exactly 114.
All inputs are finite; a program needn't handle non-finite values.
Results may differ from the reference program's by a relative error of at most 0.0001.
Values sent between devices are 32-bit elements; how exact they have to be, the bound alone decides.
A program may use at most 64 MiB of HBM per device.

```python
import math
import jax
import jax.numpy as jnp
import numpy as np
from jax import lax

M = 12
P_SIZE = 455
CAP = 114
SLOTS = 912
COLS = 128
NX = 16
ITERS = 3
N_CHAOS = 8


def draw_forcing(key, part):
    first_key, second_key, third_key = jax.random.split(key, 3)
    slot_place = jnp.arange(SLOTS, dtype=jnp.float32) / SLOTS
    row_place = jnp.arange(NX, dtype=jnp.float32) / NX
    slot_scale = jnp.exp(jax.random.uniform(second_key, (SLOTS,), jnp.float32) * math.log(10.0)) * (1.0 + 0.7 * slot_place)
    row_scale = 1.0 + 0.7 * row_place
    common = jnp.clip(jax.random.normal(third_key, (NX, COLS), jnp.float32), -2.9, 2.9)
    single = jnp.clip(jax.random.normal(first_key, (SLOTS, NX, COLS), jnp.float32), -2.9, 2.9)
    base = 0.7 * (common[None, :, :] + single)
    return base * slot_scale[:, None, None] * row_scale[None, :, None]


def levels(rng, shape, pieces, smallest, high):
    level, own = 1.0, jax.random.fold_in(rng, 6)
    for axis_at, parts in pieces:
        heights = jnp.exp(jax.random.uniform(jax.random.fold_in(own, axis_at), (parts,), jnp.float32, smallest / len(pieces), high / len(pieces)))
        level = level * jnp.repeat(heights, shape[axis_at] // parts).reshape([-1 if axis == axis_at else 1 for axis in range(len(shape))])
    return level


def profile(number_of, total, reach, lean):
    loads = [(1 << 20) // math.isqrt(grade ** lean) + 1 for grade in range(2, number_of + 1)]
    spare, holding = total - reach - (number_of - 1), [1] * (number_of - 1)
    while spare > 0:
        candidates = [i for i in range(number_of - 1) if holding[i] < reach]
        pool, budget = sum([loads[i] for i in candidates]), spare
        for i in candidates:
            extra = min(reach - holding[i], max(1, budget * loads[i] // pool), spare)
            holding[i] = holding[i] + extra
            spare = spare - extra
    return np.array([reach] + holding)


def uneven(own_key, amount, total, most, skew):
    if amount == 2:
        one = jax.random.randint(own_key, (), max(1, total - most), min(most, total - 1) + 1)
        return jnp.stack([one, total - one])
    sizes = jnp.asarray(profile(amount, total, most, skew), jnp.int32)
    twos = (amount - 1) // 2
    donor, sink = sizes[1:1 + 2 * twos:2], sizes[2:2 + 2 * twos:2]
    slack = jnp.minimum(donor - 1, most - sink)
    moved = jax.random.randint(jax.random.fold_in(own_key, 1), (twos,), 0, 1 << 20) % (slack + 1)
    sizes = sizes.at[1:1 + 2 * twos:2].set(donor - moved).at[2:2 + 2 * twos:2].set(sink + moved)
    return sizes[jax.random.permutation(jax.random.fold_in(own_key, 2), amount)]


def setup_inputs(seed: int = 0) -> dict:
    streams_of = jax.random.split(jax.random.key(seed), 5)
    forcing = draw_forcing(jax.random.fold_in(streams_of[4], 71), 0)
    mean_field = jnp.clip(jnp.exp(math.log(8.0) - 2.0794415 * jax.random.uniform(streams_of[1], (NX, COLS), jnp.float32) ** levels(streams_of[1], (NX, COLS), ((0, 4),), -0.2, 0.2)), 1.0, 8.0)
    modes = jnp.clip(0.02 + 0.030000001 * jax.random.uniform(streams_of[2], (M, NX, COLS), jnp.float32) ** levels(streams_of[2], (M, NX, COLS), ((1, 4),), -0.2, 0.2), 0.02, 0.05)
    lengths = uneven(streams_of[3], N_CHAOS, P_SIZE, CAP, 2).astype(jnp.int32)
    return {"forcing": forcing, "mean_field": mean_field, "modes": modes, "lengths": lengths}


spectrum_low = 0.05
spectrum_high = 3.0

def index_key(entry):
    return tuple((int(value) for value in entry))

def chaos_tables(terms):
    indices = [np.zeros(terms, dtype=np.int64)]
    for first in range(terms):
        entry = np.zeros(terms, dtype=np.int64)
        entry[first] += 1
        indices.append(entry)
    for first in range(terms):
        for second in range(first, terms):
            entry = np.zeros(terms, dtype=np.int64)
            entry[first] += 1
            entry[second] += 1
            indices.append(entry)
    for first in range(terms):
        for second in range(first, terms):
            for third in range(second, terms):
                entry = np.zeros(terms, dtype=np.int64)
                entry[first] += 1
                entry[second] += 1
                entry[third] += 1
                indices.append(entry)
    lookup = {}
    for number, entry in enumerate(indices):
        lookup[index_key(entry)] = number
    count = len(indices)
    upward = np.full((count, terms), count, dtype=np.int64)
    downward = np.full((count, terms), count, dtype=np.int64)
    up_coef = np.zeros((count, terms))
    down_coef = np.zeros((count, terms))
    for number, entry in enumerate(indices):
        for term in range(terms):
            if entry.sum() < 3:
                other = entry.copy()
                other[term] += 1
                upward[number, term] = lookup[index_key(other)]
                up_coef[number, term] = math.sqrt(entry[term] + 1)
            if entry[term] > 0:
                other = entry.copy()
                other[term] -= 1
                downward[number, term] = lookup[index_key(other)]
                down_coef[number, term] = math.sqrt(entry[term])
    return (upward.astype(np.int32), downward.astype(np.int32), up_coef.astype(np.float32), down_coef.astype(np.float32))

def shifted(values, toward):
    blank = jnp.zeros_like(values[..., :1])
    if toward > 0:
        return jnp.concatenate([values[..., 1:], blank], axis=-1)
    return jnp.concatenate([blank, values[..., :-1]], axis=-1)

def stiffness(field_pad, tile_pad):
    center_field = field_pad[..., 1:-1, :]
    center_tile = tile_pad[..., 1:-1, :]
    result = 0.5 * (center_field + field_pad[..., :-2, :]) * (center_tile - tile_pad[..., :-2, :])
    result = result + 0.5 * (center_field + field_pad[..., 2:, :]) * (center_tile - tile_pad[..., 2:, :])
    for toward in (1, -1):
        result = result + 0.5 * (center_field + shifted(center_field, toward)) * (center_tile - shifted(center_tile, toward))
    return result

def diagonal_of(field_pad):
    center_field = field_pad[..., 1:-1, :]
    result = 0.5 * (center_field + field_pad[..., :-2, :])
    result = result + 0.5 * (center_field + field_pad[..., 2:, :])
    for toward in (1, -1):
        result = result + 0.5 * (center_field + shifted(center_field, toward))
    return result

def pad_rows(values):
    widths = [(0, 0)] * (values.ndim - 2) + [(1, 1), (0, 0)]
    return jnp.pad(values, widths)

def reference(forcing, mean_field, modes, lengths):
    upward, downward, up_coef, down_coef = chaos_tables(M)
    up_table = jnp.asarray(upward, dtype=jnp.int32)
    down_table = jnp.asarray(downward, dtype=jnp.int32)
    up_values = jnp.asarray(up_coef, dtype=jnp.float32)
    down_values = jnp.asarray(down_coef, dtype=jnp.float32)
    slot_cap = forcing.shape[0] // N_CHAOS
    group_ends = jnp.cumsum(lengths).astype(jnp.int32)
    group_starts = (group_ends - lengths).astype(jnp.int32)
    coeff_index = jnp.arange(P_SIZE, dtype=jnp.int32)
    owner = lax.optimization_barrier(jnp.sum((coeff_index[:, None] >= group_ends[None, :]).astype(jnp.int32), axis=1)).astype(jnp.int32)
    slot_of = (owner * slot_cap + coeff_index - group_starts[owner]).astype(jnp.int32)
    rhs = forcing[slot_of]
    field_pad = pad_rows(mean_field)
    diagonal = diagonal_of(field_pad)

    def operator(tiles):
        extended = jnp.concatenate([tiles, jnp.zeros((1,) + tiles.shape[1:], jnp.float32)], axis=0)
        total = stiffness(field_pad, pad_rows(tiles))

        def one_term(carry, inputs):
            up_index, down_index, up_weight, down_weight, mode = inputs
            coupled = up_weight[:, None, None] * extended[up_index] + down_weight[:, None, None] * extended[down_index]
            return (carry + stiffness(pad_rows(mean_field * mode), pad_rows(coupled)), None)
        total, unused = lax.scan(one_term, total, (up_table.T, down_table.T, up_values.T, down_values.T, modes))
        return total
    theta = (spectrum_high + spectrum_low) / 2.0
    delta = (spectrum_high - spectrum_low) / 2.0
    sigma = theta / delta
    rho = 1.0 / sigma
    residual = rhs
    solution = jnp.zeros_like(rhs)
    direction = residual / diagonal / theta
    norm_list = []
    for sweep_index in range(ITERS):
        solution = solution + direction
        residual = residual - operator(direction)
        norm_list.append(jnp.sqrt(jnp.sum(residual * residual)))
        if sweep_index + 1 < ITERS:
            rho_new = 1.0 / (2.0 * sigma - rho)
            direction = rho_new * rho * direction + 2.0 * rho_new / delta * (residual / diagonal)
            rho = rho_new
    output = jnp.zeros_like(forcing).at[slot_of].set(solution)
    return (output, jnp.stack(norm_list))
```

```python
import functools
import math

import jax
import jax.numpy as jnp
import numpy as np
from jax import lax
from jax.experimental import pallas as pl
from jax.experimental.pallas import tpu as pltpu
from jax.sharding import PartitionSpec as P

M = 12
P_SIZE = 455
ITERS = 3
LOW = 91
LP = 96
HP = 368
NP = LP + HP
HALO = 3
SIDE = 4

spectrum_low = 0.05
spectrum_high = 3.0
F32 = jnp.float32
BF16 = jnp.bfloat16


def place(p):
    return p if p < LOW else p + (LP - LOW)


def tables():
    indices = [()]
    indices += [(a,) for a in range(M)]
    indices += [(a, b) for a in range(M) for b in range(a, M)]
    indices += [(a, b, c) for a in range(M) for b in range(a, M) for c in range(b, M)]
    lookup = {entry: number for number, entry in enumerate(indices)}
    to_low = np.zeros((M * LP, NP), np.float32)
    to_high = np.zeros((HP, M * LP), np.float32)
    scale = np.ones((NP,), np.float64)
    for number, entry in enumerate(indices):
        scale[place(number)] = math.sqrt(math.prod(math.factorial(entry.count(k)) for k in set(entry)))
        if len(entry) == 3:
            continue
        for k in range(M):
            other = lookup[tuple(sorted(entry + (k,)))]
            to_low[k * LP + number, place(other)] = entry.count(k) + 1
            if other < LOW:
                to_low[k * LP + other, place(number)] = 1.0
            else:
                to_high[place(other) - LP, k * LP + number] = 1.0
    scales = np.stack([1.0 / scale, scale]).astype(np.float32)
    scales = np.ascontiguousarray(np.broadcast_to(scales[:, :, None], (2, NP, 128)))
    return to_low, to_high, scales


def round_up(value, unit):
    return -(-value // unit) * unit


def halves(x):
    hi = x.astype(BF16)
    return hi, (x - hi.astype(F32)).astype(BF16)


def kernel(groups, tiles, cap, rows, cols, lengths_ref, forcing_ref, mean_ref, modes_ref, low_hbm, high_hbm, scale_ref,
           out_ref, norms_ref,
           low_ref, high_ref, send_ref, recv_ref, own_ref, up_ref, down_ref, field_ref, coef_ref, dinv_ref,
           hot_ref, d_ref, r_ref, s_ref, db_ref, v_ref, wb_ref, rsend_ref, rrecv_ref, part_ref, nbuf_ref, zpart_ref, zbuf_ref,
           load_sem, f_send, f_recv, h_send, h_recv, a_send, a_recv, b_send, b_recv, n_send, n_recv, z_send, z_recv):
    me = lax.axis_index("chaos")
    sp = lax.axis_index("space")
    width = cols // groups
    stride = width + 2 * SIDE
    lanes = d_ref.shape[1]
    capp = recv_ref.shape[1]
    half = rsend_ref.shape[1]
    nx = rows * tiles
    total_rows = rows + 2 * HALO
    mesh_id = pl.DeviceIdType.MESH

    load_low = pltpu.make_async_copy(low_hbm, low_ref, load_sem.at[0])
    load_high = pltpu.make_async_copy(high_hbm, high_ref, load_sem.at[1])
    load_low.start()
    load_high.start()

    barrier = pltpu.get_barrier_semaphore()

    def greet_group(j, carry):
        pl.semaphore_signal(barrier, inc=1, device_id=(sp, lax.rem(me + j, groups)), device_id_type=mesh_id)
        return carry

    def greet_column(j, carry):
        pl.semaphore_signal(barrier, inc=1, device_id=(lax.rem(sp + j, tiles), me), device_id_type=mesh_id)
        return carry

    lax.fori_loop(1, groups, greet_group, 0)
    lax.fori_loop(1, tiles, greet_column, 0)

    lane128 = lax.broadcasted_iota(jnp.int32, (cap, 128), 1)

    def pack(j, carry):
        c = lax.rem(me + j, groups)
        base = c * width - SIDE
        block = jnp.zeros((cap, 128), F32)
        for r in range(rows):
            shift = lax.rem(r * stride - base + 256, 128)
            rolled = pltpu.roll(forcing_ref[:, r, :], shift, 1)
            block = jnp.where((lane128 >= r * stride) & (lane128 < (r + 1) * stride), rolled, block)
        send_ref[j, 0:cap, :] = block
        if capp > cap:
            send_ref[j, cap:capp, :] = jnp.zeros((capp - cap, 128), F32)
        return carry

    lax.fori_loop(0, groups, pack, 0)
    field_ref[1, 0] = mean_ref[...]
    field_ref[1, 1:] = modes_ref[...]

    pl.semaphore_wait(barrier, groups - 1 + tiles - 1)

    def a2a(j):
        c = lax.rem(me + j, groups)
        return pltpu.make_async_remote_copy(
            src_ref=send_ref.at[j], dst_ref=recv_ref.at[me], send_sem=a_send.at[j], recv_sem=a_recv.at[me],
            device_id=(sp, c), device_id_type=mesh_id)

    def a2a_in(j):
        c = lax.rem(me + j, groups)
        return pltpu.make_async_remote_copy(
            src_ref=send_ref.at[j], dst_ref=recv_ref.at[c], send_sem=a_send.at[j], recv_sem=a_recv.at[c],
            device_id=(sp, c), device_id_type=mesh_id)

    def start_a2a(j, carry):
        a2a(j).start()
        return carry

    lax.fori_loop(1, groups, start_a2a, 0)

    def column(src, dst, send, recv, target):
        return pltpu.make_async_remote_copy(
            src_ref=src, dst_ref=dst, send_sem=send, recv_sem=recv, device_id=(target, me), device_id_type=mesh_id)

    up_target = lax.rem(sp + tiles - 1, tiles)
    down_target = lax.rem(sp + 1, tiles)
    has_up = sp > 0
    has_down = sp < tiles - 1
    f_up = column(field_ref.at[1], field_ref.at[2], f_send.at[0], f_recv.at[1], up_target)
    f_down = column(field_ref.at[1], field_ref.at[0], f_send.at[1], f_recv.at[0], down_target)
    f_from_up = column(field_ref.at[1], field_ref.at[0], f_send.at[0], f_recv.at[0], up_target)
    f_from_down = column(field_ref.at[1], field_ref.at[2], f_send.at[1], f_recv.at[1], down_target)

    @pl.when(has_up)
    def _():
        f_up.start()

    @pl.when(has_down)
    def _():
        f_down.start()

    recv_ref[me] = send_ref[0]

    slots = groups * capp
    slot = lax.broadcasted_iota(jnp.int32, (1, slots), 1)
    coef = jnp.full((1, slots), -1, jnp.int32)
    start = jnp.int32(0)
    starts = []
    for g in range(groups):
        count = lengths_ref[g]
        here = slot - g * capp
        coef = jnp.where((here >= 0) & (here < count), start + here, coef)
        starts.append(start)
        start = start + count
    row = lax.broadcasted_iota(jnp.int32, (NP, slots), 0)
    row_coef = jnp.where(row < LOW, row, jnp.where(row < LP, -2, row - (LP - LOW)))
    hot_ref[...] = jnp.where(row_coef == coef, 1.0, 0.0).astype(BF16)

    @pl.when(jnp.logical_not(has_up))
    def _():
        field_ref[0] = jnp.zeros(field_ref.shape[1:], F32)
        up_ref[...] = jnp.zeros(up_ref.shape, F32)

    @pl.when(jnp.logical_not(has_down))
    def _():
        field_ref[2] = jnp.zeros(field_ref.shape[1:], F32)
        down_ref[...] = jnp.zeros(down_ref.shape, F32)

    @pl.when(has_up)
    def _():
        f_up.wait_send()
        f_from_up.wait_recv()

    @pl.when(has_down)
    def _():
        f_down.wait_send()
        f_from_down.wait_recv()

    base = me * width - SIDE
    n_fields = M + 1
    lane_f = lax.broadcasted_iota(jnp.int32, (n_fields, lanes), 1)
    col_f = lax.broadcasted_iota(jnp.int32, (n_fields, cols), 1)
    first_field = lax.broadcasted_iota(jnp.int32, (n_fields, cols), 0) == 0

    def field_row(g):
        x = field_ref[g // rows, :, g % rows, :]
        return jnp.where(first_field, x, x * x[0:1, :])

    skip = rows - HALO - 1
    fields = [field_row(skip + g) for g in range(total_rows + 2)]
    packed = [jnp.zeros((n_fields, lanes), F32) for _ in range(4)]
    valid = jnp.zeros((1, lanes), jnp.bool_)
    lane1 = lax.broadcasted_iota(jnp.int32, (1, lanes), 1)
    for r in range(total_rows):
        here = fields[r + 1]
        east = jnp.where(col_f < cols - 1, pltpu.roll(here, cols - 1, 1), 0.0)
        west = jnp.where(col_f > 0, pltpu.roll(here, 1, 1), 0.0)
        shift = lax.rem(r * stride - base + 512, 128)
        at = lane1 - r * stride
        inside = ((at >= 0) & (at < stride) & (at + base >= 0) & (at + base < cols)
                  & (sp * rows - HALO + r >= 0) & (sp * rows - HALO + r < nx))
        valid = valid | inside
        for n, other in enumerate((east, west, fields[r + 2], fields[r])):
            rolled = pltpu.roll(0.5 * (here + other), shift, 1)
            if lanes > 128:
                rolled = jnp.concatenate([rolled] * (lanes // 128), axis=1)
            packed[n] = jnp.where(inside, rolled, packed[n])
    for n in range(4):
        coef_ref[n] = packed[n]
    diagonal = packed[0][0:1] + packed[1][0:1] + packed[2][0:1] + packed[3][0:1]
    dinv_ref[...] = jnp.where(valid, 1.0 / jnp.where(valid, diagonal, 1.0), 0.0)

    def wait_a2a(j, carry):
        a2a(j).wait_send()
        a2a_in(j).wait_recv()
        return carry

    lax.fori_loop(1, groups, wait_a2a, 0)
    hi, lo = halves(recv_ref[...].reshape(slots, 128))
    both = jnp.dot(hot_ref[...], jnp.concatenate([hi, lo], axis=1), preferred_element_type=F32)
    own_ref[...] = (both[:, :128] + both[:, 128:]) * scale_ref[0]

    h_up = column(own_ref, down_ref, h_send.at[0], h_recv.at[1], up_target)
    h_down = column(own_ref, up_ref, h_send.at[1], h_recv.at[0], down_target)
    h_from_up = column(own_ref, up_ref, h_send.at[0], h_recv.at[0], up_target)
    h_from_down = column(own_ref, down_ref, h_send.at[1], h_recv.at[1], down_target)

    @pl.when(has_up)
    def _():
        h_up.start()

    @pl.when(has_down)
    def _():
        h_down.start()

    @pl.when(has_up)
    def _():
        h_up.wait_send()
        h_from_up.wait_recv()

    @pl.when(has_down)
    def _():
        h_down.wait_send()
        h_from_down.wait_recv()

    lane_n = lax.broadcasted_iota(jnp.int32, (NP, 128), 1)

    def spread(block, lower, upper, shift):
        block = jnp.where((lane_n >= lower) & (lane_n < upper), block, 0.0)
        if lanes > 128:
            block = jnp.concatenate([block, jnp.zeros((NP, lanes - 128), F32)], axis=1)
        return pltpu.roll(block, shift % lanes, 1)

    above = (rows - HALO) * stride
    r0 = spread(own_ref[...], 0, rows * stride, HALO * stride)
    r0 = r0 + spread(up_ref[...], above, rows * stride, -above)
    r0 = r0 + spread(down_ref[...], 0, HALO * stride, (HALO + rows) * stride)
    r_ref[...] = r0

    theta = (spectrum_high + spectrum_low) / 2.0
    delta = (spectrum_high - spectrum_low) / 2.0
    sigma = theta / delta
    rho = 1.0 / sigma
    d_ref[...] = r0 * (dinv_ref[...] * (1.0 / theta))
    s_ref[...] = d_ref[...]

    own_lane = jnp.zeros((1, lanes), jnp.bool_)
    for r in range(rows):
        at = lane1 - (HALO + r) * stride - SIDE
        own_lane = own_lane | ((at >= 0) & (at < width))
    own_f = jnp.where(own_lane, 1.0, 0.0)

    load_low.wait()
    load_high.wait()
    part_ref[...] = jnp.zeros(part_ref.shape, F32)

    def neighbours(x):
        return (pltpu.roll(x, lanes - 1, 1), pltpu.roll(x, 1, 1),
                pltpu.roll(x, lanes - stride, 1), pltpu.roll(x, stride, 1))

    CH = 16

    def split_rows(i, carry):
        at = pl.multiple_of(i * CH, CH)
        hi, lo = halves(d_ref[pl.ds(at, CH), :])
        db_ref[pl.ds(at, CH), 0:lanes] = hi
        db_ref[pl.ds(at, CH), lanes:] = lo
        return carry

    def low_terms(i, carry):
        at = pl.multiple_of(i * CH, CH)
        x = d_ref[pl.ds(at, CH), :]
        diffs = [x - y for y in neighbours(x)]
        for k in range(M):
            w = coef_ref[0, k + 1:k + 2, :] * diffs[0]
            for n in range(1, 4):
                w = w + coef_ref[n, k + 1:k + 2, :] * diffs[n]
            hi, lo = halves(w)
            there = pl.multiple_of(k * LP + at, CH)
            wb_ref[pl.ds(there, CH), 0:lanes] = hi
            wb_ref[pl.ds(there, CH), lanes:] = lo
        return carry

    def low_result(i, carry):
        at = pl.multiple_of(i * CH, CH)
        x = d_ref[pl.ds(at, CH), :]
        sums = [coef_ref[n, 0:1, :] * x for n in range(4)]
        for k in range(M):
            there = pl.multiple_of(k * LP + at, CH)
            v = v_ref[pl.ds(there, CH), 0:lanes] + v_ref[pl.ds(there, CH), lanes:]
            for n in range(4):
                sums[n] = sums[n] + coef_ref[n, k + 1:k + 2, :] * v
        result = (sums[0] + sums[1]) + (sums[2] + sums[3])
        result = result - pltpu.roll(sums[0], 1, 1) - pltpu.roll(sums[1], lanes - 1, 1)
        result = result - pltpu.roll(sums[2], stride, 1) - pltpu.roll(sums[3], lanes - stride, 1)
        r_ref[pl.ds(at, CH), :] = r_ref[pl.ds(at, CH), :] - result
        return carry

    def high_result(i, carry):
        at = pl.multiple_of(i * CH, CH)
        x = d_ref[pl.ds(LP + at, CH), :]
        result = v_ref[pl.ds(at, CH), 0:lanes] + v_ref[pl.ds(at, CH), lanes:]
        for n, y in enumerate(neighbours(x)):
            result = result + coef_ref[n, 0:1, :] * (x - y)
        r_ref[pl.ds(LP + at, CH), :] = r_ref[pl.ds(LP + at, CH), :] - result
        return carry

    def back(j):
        c = lax.rem(me + j, groups)
        return pltpu.make_async_remote_copy(
            src_ref=rsend_ref.at[c], dst_ref=rrecv_ref.at[me], send_sem=b_send.at[j], recv_sem=b_recv.at[me],
            device_id=(sp, c), device_id_type=mesh_id)

    def back_in(j):
        c = lax.rem(me + j, groups)
        return pltpu.make_async_remote_copy(
            src_ref=rsend_ref.at[c], dst_ref=rrecv_ref.at[c], send_sem=b_send.at[j], recv_sem=b_recv.at[c],
            device_id=(sp, c), device_id_type=mesh_id)

    def send_back():
        piece = rows * width
        s = s_ref[...]
        q1 = jnp.zeros((NP, 128), F32)
        q2 = jnp.zeros((NP, 128), F32)
        for r in range(rows):
            origin = (HALO + r) * stride + SIDE
            a = pltpu.roll(s, (r * width - origin) % lanes, 1)[:, :128]
            b = pltpu.roll(s, (piece + r * width - origin) % lanes, 1)[:, :128]
            q1 = jnp.where((lane_n >= r * width) & (lane_n < (r + 1) * width), a, q1)
            q2 = jnp.where((lane_n >= piece + r * width) & (lane_n < piece + (r + 1) * width), b, q2)
        p_lane = lax.broadcasted_iota(jnp.int32, (half, NP), 1)
        p_coef = jnp.where(p_lane < LOW, p_lane, jnp.where(p_lane < LP, -2, p_lane - (LP - LOW)))
        t = lax.broadcasted_iota(jnp.int32, (half, NP), 0)
        operands = []
        for q in (q1, q2):
            hi, lo = halves(q * scale_ref[1])
            operands.append(jnp.concatenate([hi, lo], axis=1))
        for g in range(groups):
            block = None
            for h in range(2):
                tt = t + h * half
                hot = jnp.where((tt < lengths_ref[g]) & (p_coef == starts[g] + tt), 1.0, 0.0).astype(BF16)
                term = jnp.dot(hot, operands[h], preferred_element_type=F32)
                block = term if block is None else block + term
            rsend_ref[g] = block[:, :128] + block[:, 128:]

        def start_back(j, carry):
            back(j).start()
            return carry

        lax.fori_loop(1, groups, start_back, 0)
        rrecv_ref[me] = rsend_ref[me]

    weight = scale_ref[1] * scale_ref[1]
    if lanes > 128:
        weight = jnp.concatenate([weight] * (lanes // 128), axis=1)
    for step in range(ITERS):
        lax.fori_loop(0, NP // CH, split_rows, 0)
        lax.fori_loop(0, LP // CH, low_terms, 0)
        v_ref[...] = jnp.dot(low_ref[...], db_ref[...], preferred_element_type=F32)
        lax.fori_loop(0, LP // CH, low_result, 0)
        v_ref[0:HP, :] = jnp.dot(high_ref[...], wb_ref[...], preferred_element_type=F32)
        lax.fori_loop(0, HP // CH, high_result, 0)
        res = r_ref[...]
        part = jnp.sum(res * res * weight, axis=0, keepdims=True) * own_f
        folded = part[:, 0:128]
        for extra in range(1, lanes // 128):
            folded = folded + part[:, extra * 128:(extra + 1) * 128]
        part_ref[step:step + 1, :] = folded
        if step + 1 < ITERS:
            rho_new = 1.0 / (2.0 * sigma - rho)
            new = (rho_new * rho) * d_ref[...] + (2.0 * rho_new / delta) * (res * dinv_ref[...])
            d_ref[...] = new
            s_ref[...] = s_ref[...] + new
            rho = rho_new
            if step + 2 == ITERS:
                send_back()

    def norm_copy(j, slot):
        c = lax.rem(me + j, groups)
        return pltpu.make_async_remote_copy(
            src_ref=part_ref, dst_ref=nbuf_ref.at[c if slot else me], send_sem=n_send.at[j],
            recv_sem=n_recv.at[c if slot else me], device_id=(sp, c), device_id_type=mesh_id)

    def z_copy(j, slot):
        z = lax.rem(sp + j, tiles)
        return pltpu.make_async_remote_copy(
            src_ref=zpart_ref, dst_ref=zbuf_ref.at[z if slot else sp], send_sem=z_send.at[j],
            recv_sem=z_recv.at[z if slot else sp], device_id=(z, me), device_id_type=mesh_id)

    def n_start(j, carry):
        norm_copy(j, False).start()
        return carry

    def n_wait(j, carry):
        norm_copy(j, False).wait_send()
        norm_copy(j, True).wait_recv()
        return carry

    def z_start(j, carry):
        z_copy(j, False).start()
        return carry

    def z_wait(j, carry):
        z_copy(j, False).wait_send()
        z_copy(j, True).wait_recv()
        return carry

    def back_wait(j, carry):
        back(j).wait_send()
        back_in(j).wait_recv()
        return carry

    lax.fori_loop(1, groups, n_start, 0)
    nbuf_ref[me] = part_ref[...]
    lax.fori_loop(1, groups, n_wait, 0)
    zpart_ref[...] = jnp.sum(nbuf_ref[...], axis=0)
    lax.fori_loop(1, tiles, z_start, 0)
    zbuf_ref[sp] = zpart_ref[...]

    lax.fori_loop(1, groups, back_wait, 0)
    piece = rows * width
    lane_h = lax.broadcasted_iota(jnp.int32, (half, 128), 1)
    for h in range(2):
        count = min(half, cap - h * half)
        for r in range(rows):
            block = jnp.zeros((half, 128), F32)
            for c in range(groups):
                rolled = pltpu.roll(rrecv_ref[c], (c * width - h * piece - r * width) % 128, 1)
                block = jnp.where((lane_h >= c * width) & (lane_h < (c + 1) * width), rolled, block)
            out_ref[h * half:h * half + count, r, :] = block[0:count]

    lax.fori_loop(1, tiles, z_wait, 0)
    total = jnp.sum(jnp.sum(zbuf_ref[...], axis=0), axis=1, keepdims=True)
    norms_ref[...] = jnp.broadcast_to(jnp.sqrt(total), norms_ref.shape)


def local(groups, tiles, forcing, mean_field, modes, lengths):
    cap, rows, cols = forcing.shape
    width = cols // groups
    stride = width + 2 * SIDE
    lanes = round_up((rows + 2 * HALO) * stride, 128)
    capp = round_up(cap, 8)
    half = round_up(-(-cap // 2), 16)
    low, high, scales = tables()
    vmem = pl.BlockSpec(memory_space=pltpu.VMEM)
    hbm = pl.BlockSpec(memory_space=pl.ANY)
    dma = pltpu.SemaphoreType.DMA
    out, norms = pl.pallas_call(
        functools.partial(kernel, groups, tiles, cap, rows, cols),
        out_shape=(jax.ShapeDtypeStruct((cap, rows, cols), F32), jax.ShapeDtypeStruct((8, 128), F32)),
        in_specs=[pl.BlockSpec(memory_space=pltpu.SMEM), vmem, vmem, vmem, hbm, hbm, vmem],
        out_specs=(vmem, vmem),
        scratch_shapes=[
            pltpu.VMEM((M * LP, NP), BF16), pltpu.VMEM((HP, M * LP), BF16),
            pltpu.VMEM((groups, capp, 128), F32), pltpu.VMEM((groups, capp, 128), F32),
            pltpu.VMEM((NP, 128), F32), pltpu.VMEM((NP, 128), F32), pltpu.VMEM((NP, 128), F32),
            pltpu.VMEM((3, M + 1, rows, cols), F32), pltpu.VMEM((4, M + 1, lanes), F32), pltpu.VMEM((1, lanes), F32),
            pltpu.VMEM((NP, groups * capp), BF16),
            pltpu.VMEM((NP, lanes), F32), pltpu.VMEM((NP, lanes), F32), pltpu.VMEM((NP, lanes), F32),
            pltpu.VMEM((NP, 2 * lanes), BF16), pltpu.VMEM((M * LP, 2 * lanes), F32), pltpu.VMEM((M * LP, 2 * lanes), BF16),
            pltpu.VMEM((groups, half, 128), F32), pltpu.VMEM((groups, half, 128), F32),
            pltpu.VMEM((8, 128), F32), pltpu.VMEM((groups, 8, 128), F32),
            pltpu.VMEM((8, 128), F32), pltpu.VMEM((tiles, 8, 128), F32),
            dma((2,)), dma((2,)), dma((2,)), dma((2,)), dma((2,)),
            dma((groups,)), dma((groups,)), dma((groups,)), dma((groups,)),
            dma((groups,)), dma((groups,)), dma((tiles,)), dma((tiles,)),
        ],
        compiler_params=pltpu.CompilerParams(collective_id=0, has_side_effects=True, vmem_limit_bytes=48 * 2**20),
        name="chebyshev",
    )(lengths, forcing, mean_field, modes, jnp.asarray(low, BF16), jnp.asarray(high, BF16), jnp.asarray(scales))
    return out, norms[:ITERS, 0]


def solution(mesh):
    in_specs = (P("chaos", "space", None), P("space", None), P(None, "space", None), P())
    out_specs = (P("chaos", "space", None), P())
    body = functools.partial(local, mesh.shape["chaos"], mesh.shape["space"])
    return jax.shard_map(body, mesh=mesh, in_specs=in_specs, out_specs=out_specs, check_vma=False)
```

```python
import functools
import math

import jax
import jax.numpy as jnp
import numpy as np
from jax import lax
from jax.experimental import pallas as pl
from jax.experimental.pallas import tpu as pltpu
from jax.sharding import PartitionSpec as P

M = 12
P_SIZE = 455
ITERS = 3
LOW = 91
LP = 96
HP = 368
NP = LP + HP
HALO = 3
SIDE = 4

spectrum_low = 0.05
spectrum_high = 3.0
F32 = jnp.float32
BF16 = jnp.bfloat16


def place(p):
    return p if p < LOW else p + (LP - LOW)


def tables():
    indices = [()]
    indices += [(a,) for a in range(M)]
    indices += [(a, b) for a in range(M) for b in range(a, M)]
    indices += [(a, b, c) for a in range(M) for b in range(a, M) for c in range(b, M)]
    lookup = {entry: number for number, entry in enumerate(indices)}
    to_low = np.zeros((M * LP, NP), np.float32)
    to_high = np.zeros((HP, M * LP), np.float32)
    scale = np.ones((NP,), np.float64)
    for number, entry in enumerate(indices):
        scale[place(number)] = math.sqrt(math.prod(math.factorial(entry.count(k)) for k in set(entry)))
        if len(entry) == 3:
            continue
        for k in range(M):
            other = lookup[tuple(sorted(entry + (k,)))]
            to_low[k * LP + number, place(other)] = entry.count(k) + 1
            if other < LOW:
                to_low[k * LP + other, place(number)] = 1.0
            else:
                to_high[place(other) - LP, k * LP + number] = 1.0
    scales = np.stack([1.0 / scale, scale]).astype(np.float32)
    scales = np.ascontiguousarray(np.broadcast_to(scales[:, :, None], (2, NP, 128)))
    return to_low, to_high, scales


def round_up(value, unit):
    return -(-value // unit) * unit


def halves(x):
    hi = x.astype(BF16)
    return hi, (x - hi.astype(F32)).astype(BF16)


def kernel(groups, tiles, cap, rows, cols, lengths_ref, forcing_hbm, mean_hbm, modes_hbm, low_hbm, high_hbm, scale_hbm,
           out_ref, norms_ref,
           low_ref, high_ref, scale_ref, forcing_ref, send_ref, recv_ref, own_ref, to_up_ref, to_down_ref, up_ref, down_ref, field_ref, coef_ref, dinv_ref,
           hot_ref, back_ref, d_ref, r_ref, s_ref, db_ref, v_ref, h_ref, wb_ref, rsend_ref, rrecv_ref, part_ref, nbuf_ref, zpart_ref, zbuf_ref,
           load_sem, f_send, f_recv, h_send, h_recv, a_send, a_recv, b_send, b_recv, n_send, n_recv, z_send, z_recv):
    me = lax.axis_index("chaos")
    sp = lax.axis_index("space")
    width = cols // groups
    stride = width + 2 * SIDE
    lanes = d_ref.shape[1]
    capp = recv_ref.shape[1]
    half = rsend_ref.shape[1]
    nx = rows * tiles
    total_rows = rows + 2 * HALO
    mesh_id = pl.DeviceIdType.MESH

    loads = [pltpu.make_async_copy(src, dst, load_sem.at[n]) for n, (src, dst) in enumerate((
        (forcing_hbm, forcing_ref), (mean_hbm, field_ref.at[1, 0]), (modes_hbm, field_ref.at[1, 1:]),
        (scale_hbm, scale_ref), (low_hbm, low_ref), (high_hbm, high_ref)))]
    for load in loads:
        load.start()

    barrier = pltpu.get_barrier_semaphore()

    def greet_group(j, carry):
        pl.semaphore_signal(barrier, inc=1, device_id=(sp, lax.rem(me + j, groups)), device_id_type=mesh_id)
        return carry

    def greet_column(j, carry):
        pl.semaphore_signal(barrier, inc=1, device_id=(lax.rem(sp + j, tiles), me), device_id_type=mesh_id)
        return carry

    lax.fori_loop(1, groups, greet_group, 0)
    lax.fori_loop(1, tiles, greet_column, 0)

    lane128 = lax.broadcasted_iota(jnp.int32, (cap, 128), 1)

    def pack(j, carry):
        c = lax.rem(me + j, groups)
        base = c * width - SIDE
        block = jnp.zeros((cap, 128), F32)
        for r in range(rows):
            shift = lax.rem(r * stride - base + 256, 128)
            rolled = pltpu.roll(forcing_ref[:, r, :], shift, 1)
            block = jnp.where((lane128 >= r * stride) & (lane128 < (r + 1) * stride), rolled, block)
        send_ref[j, 0:cap, :] = block
        if capp > cap:
            send_ref[j, cap:capp, :] = jnp.zeros((capp - cap, 128), F32)
        return carry

    def a2a(j):
        c = lax.rem(me + j, groups)
        return pltpu.make_async_remote_copy(
            src_ref=send_ref.at[j], dst_ref=recv_ref.at[me], send_sem=a_send.at[j], recv_sem=a_recv.at[me],
            device_id=(sp, c), device_id_type=mesh_id)

    def a2a_in(j):
        c = lax.rem(me + j, groups)
        return pltpu.make_async_remote_copy(
            src_ref=send_ref.at[j], dst_ref=recv_ref.at[c], send_sem=a_send.at[j], recv_sem=a_recv.at[c],
            device_id=(sp, c), device_id_type=mesh_id)

    def start_a2a(j, carry):
        a2a(j).start()
        return carry

    def pack_and_start(j, carry):
        pack(j, carry)
        a2a(j).start()
        return carry

    early = min(4, groups)
    loads[0].wait()
    for j in range(early):
        pack(j, 0)
    pl.semaphore_wait(barrier, groups - 1 + tiles - 1)
    lax.fori_loop(1, early, start_a2a, 0)
    loads[1].wait()
    loads[2].wait()

    def column(src, dst, send, recv, target):
        return pltpu.make_async_remote_copy(
            src_ref=src, dst_ref=dst, send_sem=send, recv_sem=recv, device_id=(target, me), device_id_type=mesh_id)

    up_target = lax.rem(sp + tiles - 1, tiles)
    down_target = lax.rem(sp + 1, tiles)
    has_up = sp > 0
    has_down = sp < tiles - 1
    f_up = column(field_ref.at[1], field_ref.at[2], f_send.at[0], f_recv.at[1], up_target)
    f_down = column(field_ref.at[1], field_ref.at[0], f_send.at[1], f_recv.at[0], down_target)
    f_from_up = column(field_ref.at[1], field_ref.at[0], f_send.at[0], f_recv.at[0], up_target)
    f_from_down = column(field_ref.at[1], field_ref.at[2], f_send.at[1], f_recv.at[1], down_target)

    @pl.when(has_up)
    def _():
        f_up.start()

    @pl.when(has_down)
    def _():
        f_down.start()

    lax.fori_loop(early, groups, pack_and_start, 0, unroll=groups <= 8)
    recv_ref[me] = send_ref[0]

    slots = groups * capp
    slot = lax.broadcasted_iota(jnp.int32, (1, slots), 1)
    coef = jnp.full((1, slots), -1, jnp.int32)
    start = jnp.int32(0)
    starts = []
    for g in range(groups):
        count = lengths_ref[g]
        here = slot - g * capp
        coef = jnp.where((here >= 0) & (here < count), start + here, coef)
        starts.append(start)
        start = start + count
    row = lax.broadcasted_iota(jnp.int32, (NP, slots), 0)
    row_coef = jnp.where(row < LOW, row, jnp.where(row < LP, -2, row - (LP - LOW)))
    hot_ref[...] = jnp.where(row_coef == coef, 1.0, 0.0).astype(BF16)
    p_lane = lax.broadcasted_iota(jnp.int32, (half, NP), 1)
    p_coef = jnp.where(p_lane < LOW, p_lane, jnp.where(p_lane < LP, -2, p_lane - (LP - LOW)))
    t = lax.broadcasted_iota(jnp.int32, (half, NP), 0)
    for h in range(2):
        tt = t + h * half
        for g in range(groups):
            hot = jnp.where((tt < lengths_ref[g]) & (p_coef - tt == starts[g]), 1.0, 0.0).astype(BF16)
            back_ref[h, g * half:(g + 1) * half, :] = hot

    @pl.when(jnp.logical_not(has_up))
    def _():
        field_ref[0] = jnp.zeros(field_ref.shape[1:], F32)
        up_ref[...] = jnp.zeros(up_ref.shape, F32)

    @pl.when(jnp.logical_not(has_down))
    def _():
        field_ref[2] = jnp.zeros(field_ref.shape[1:], F32)
        down_ref[...] = jnp.zeros(down_ref.shape, F32)

    @pl.when(has_up)
    def _():
        f_up.wait_send()
        f_from_up.wait_recv()

    @pl.when(has_down)
    def _():
        f_down.wait_send()
        f_from_down.wait_recv()

    base = me * width - SIDE
    n_fields = M + 1
    lane_f = lax.broadcasted_iota(jnp.int32, (n_fields, lanes), 1)
    col_f = lax.broadcasted_iota(jnp.int32, (n_fields, cols), 1)
    first_field = lax.broadcasted_iota(jnp.int32, (n_fields, cols), 0) == 0

    def field_row(g):
        x = field_ref[g // rows, :, g % rows, :]
        return jnp.where(first_field, x, x * x[0:1, :])

    skip = rows - HALO - 1
    fields = [field_row(skip + g) for g in range(total_rows + 2)]
    packed = [jnp.zeros((n_fields, lanes), F32) for _ in range(4)]
    valid = jnp.zeros((1, lanes), jnp.bool_)
    lane1 = lax.broadcasted_iota(jnp.int32, (1, lanes), 1)
    for r in range(total_rows):
        here = fields[r + 1]
        east = jnp.where(col_f < cols - 1, pltpu.roll(here, cols - 1, 1), 0.0)
        west = jnp.where(col_f > 0, pltpu.roll(here, 1, 1), 0.0)
        shift = lax.rem(r * stride - base + 512, 128)
        at = lane1 - r * stride
        inside = ((at >= 0) & (at < stride) & (at + base >= 0) & (at + base < cols)
                  & (sp * rows - HALO + r >= 0) & (sp * rows - HALO + r < nx))
        valid = valid | inside
        for n, other in enumerate((east, west, fields[r + 2], fields[r])):
            rolled = pltpu.roll(0.5 * (here + other), shift, 1)
            if lanes > 128:
                rolled = jnp.concatenate([rolled] * (lanes // 128), axis=1)
            packed[n] = jnp.where(inside, rolled, packed[n])
    for n in range(4):
        coef_ref[n] = packed[n]
    diagonal = packed[0][0:1] + packed[1][0:1] + packed[2][0:1] + packed[3][0:1]
    dinv_ref[...] = jnp.where(valid, 1.0 / jnp.where(valid, diagonal, 1.0), 0.0)

    def wait_a2a(j, carry):
        a2a(j).wait_send()
        a2a_in(j).wait_recv()
        return carry

    lax.fori_loop(1, groups, wait_a2a, 0)
    hi, lo = halves(recv_ref[...].reshape(slots, 128))
    both = jnp.dot(hot_ref[...], jnp.concatenate([hi, lo], axis=1), preferred_element_type=F32)
    loads[3].wait()
    own = (both[:, :128] + both[:, 128:]) * scale_ref[0]
    own_ref[...] = own

    np2 = NP // 2
    lane_2 = lax.broadcasted_iota(jnp.int32, (np2, 128), 1)
    segments = []
    offset = 0
    for e in range(1, HALO + 1):
        segments.append((e, offset, width + 2 * (HALO - e), SIDE - (HALO - e)))
        offset += width + 2 * (HALO - e)

    def pack_halo(row_at):
        block = jnp.zeros((np2, 128), F32)
        for part in range(2):
            source = own[part * np2:(part + 1) * np2]
            for e, offset, size, column_at in segments:
                target = part * 64 + offset
                rolled = pltpu.roll(source, (target - row_at(e) * stride - column_at) % 128, 1)
                block = jnp.where((lane_2 >= target) & (lane_2 < target + size), rolled, block)
        return block

    to_up_ref[...] = pack_halo(lambda e: e - 1)
    to_down_ref[...] = pack_halo(lambda e: rows - e)

    h_up = column(to_up_ref, down_ref, h_send.at[0], h_recv.at[1], up_target)
    h_down = column(to_down_ref, up_ref, h_send.at[1], h_recv.at[0], down_target)
    h_from_up = column(to_down_ref, up_ref, h_send.at[0], h_recv.at[0], up_target)
    h_from_down = column(to_up_ref, down_ref, h_send.at[1], h_recv.at[1], down_target)

    @pl.when(has_up)
    def _():
        h_up.start()

    @pl.when(has_down)
    def _():
        h_down.start()

    @pl.when(has_up)
    def _():
        h_up.wait_send()
        h_from_up.wait_recv()

    @pl.when(has_down)
    def _():
        h_down.wait_send()
        h_from_down.wait_recv()

    lane_n = lax.broadcasted_iota(jnp.int32, (NP, 128), 1)

    lane_w = lax.broadcasted_iota(jnp.int32, (np2, lanes), 1)

    def wide(block, shift):
        block = pltpu.roll(block, shift % 128, 1)
        return jnp.concatenate([block] * (lanes // 128), axis=1) if lanes > 128 else block

    def assemble(part):
        mine = wide(own_ref[part * np2:(part + 1) * np2, :], HALO * stride)
        block = jnp.where((lane_w >= HALO * stride) & (lane_w < (HALO + rows) * stride), mine, 0.0)
        for source, row_at in ((up_ref[...], lambda e: HALO - e), (down_ref[...], lambda e: HALO + rows - 1 + e)):
            for e, offset, size, column_at in segments:
                target = row_at(e) * stride + column_at
                moved = wide(source, target - part * 64 - offset)
                block = jnp.where((lane_w >= target) & (lane_w < target + size), moved, block)
        return block

    theta = (spectrum_high + spectrum_low) / 2.0
    delta = (spectrum_high - spectrum_low) / 2.0
    sigma = theta / delta
    rho = 1.0 / sigma
    for part in range(2):
        here = slice(part * np2, (part + 1) * np2)
        first = assemble(part)
        r_ref[here, :] = first
        first = first * (dinv_ref[...] * (1.0 / theta))
        d_ref[here, :] = first
        s_ref[here, :] = first
        hi, lo = halves(first)
        db_ref[here, 0:lanes] = hi
        db_ref[here, lanes:] = lo

    own_lane = jnp.zeros((1, lanes), jnp.bool_)
    for r in range(rows):
        at = lane1 - (HALO + r) * stride - SIDE
        own_lane = own_lane | ((at >= 0) & (at < width))
    own_f = jnp.where(own_lane, 1.0, 0.0)

    loads[4].wait()
    loads[5].wait()
    part_ref[...] = jnp.zeros(part_ref.shape, F32)

    def neighbours(x):
        return (pltpu.roll(x, lanes - 1, 1), pltpu.roll(x, 1, 1),
                pltpu.roll(x, lanes - stride, 1), pltpu.roll(x, stride, 1))

    CH = 16

    def low_terms(at):
        x = d_ref[at:at + CH, :]
        diffs = [x - y for y in neighbours(x)]
        for k in range(M):
            w = coef_ref[0, k + 1:k + 2, :] * diffs[0]
            for n in range(1, 4):
                w = w + coef_ref[n, k + 1:k + 2, :] * diffs[n]
            hi, lo = halves(w)
            wb_ref[k * LP + at:k * LP + at + CH, 0:lanes] = hi
            wb_ref[k * LP + at:k * LP + at + CH, lanes:] = lo

    def low_result(at):
        x = d_ref[at:at + CH, :]
        sums = [coef_ref[n, 0:1, :] * x for n in range(4)]
        for k in range(M):
            there = k * LP + at
            v = v_ref[there:there + CH, 0:lanes] + v_ref[there:there + CH, lanes:]
            for n in range(4):
                sums[n] = sums[n] + coef_ref[n, k + 1:k + 2, :] * v
        result = (sums[0] + sums[1]) + (sums[2] + sums[3])
        result = result - pltpu.roll(sums[0], 1, 1) - pltpu.roll(sums[1], lanes - 1, 1)
        return x, result - pltpu.roll(sums[2], stride, 1) - pltpu.roll(sums[3], lanes - stride, 1)

    def high_result(at):
        x = d_ref[LP + at:LP + at + CH, :]
        result = h_ref[at:at + CH, 0:lanes] + h_ref[at:at + CH, lanes:]
        for n, y in enumerate(neighbours(x)):
            result = result + coef_ref[n, 0:1, :] * (x - y)
        return x, result

    def finish(at, x, result, factors):
        residual = r_ref[at:at + CH, :] - result
        scale = scale_ref[1, at:at + CH, :]
        if lanes > 128:
            scale = jnp.concatenate([scale] * (lanes // 128), axis=1)
        scaled = residual * scale
        if factors is not None:
            r_ref[at:at + CH, :] = residual
            new = factors[0] * x + factors[1] * (residual * dinv_ref[...])
            d_ref[at:at + CH, :] = new
            s_ref[at:at + CH, :] = s_ref[at:at + CH, :] + new
            hi, lo = halves(new)
            db_ref[at:at + CH, 0:lanes] = hi
            db_ref[at:at + CH, lanes:] = lo
        return scaled * scaled

    def back(j):
        c = lax.rem(me + j, groups)
        return pltpu.make_async_remote_copy(
            src_ref=rsend_ref.at[c], dst_ref=rrecv_ref.at[me], send_sem=b_send.at[j], recv_sem=b_recv.at[me],
            device_id=(sp, c), device_id_type=mesh_id)

    def back_in(j):
        c = lax.rem(me + j, groups)
        return pltpu.make_async_remote_copy(
            src_ref=rsend_ref.at[c], dst_ref=rrecv_ref.at[c], send_sem=b_send.at[j], recv_sem=b_recv.at[c],
            device_id=(sp, c), device_id_type=mesh_id)

    def send_back():
        piece = rows * width
        s = s_ref[...]
        q1 = jnp.zeros((NP, 128), F32)
        q2 = jnp.zeros((NP, 128), F32)
        for r in range(rows):
            origin = (HALO + r) * stride + SIDE
            a = pltpu.roll(s, (r * width - origin) % lanes, 1)[:, :128]
            b = pltpu.roll(s, (piece + r * width - origin) % lanes, 1)[:, :128]
            q1 = jnp.where((lane_n >= r * width) & (lane_n < (r + 1) * width), a, q1)
            q2 = jnp.where((lane_n >= piece + r * width) & (lane_n < piece + (r + 1) * width), b, q2)
        block = None
        for h, q in enumerate((q1, q2)):
            hi, lo = halves(q * scale_ref[1])
            term = jnp.dot(back_ref[h], jnp.concatenate([hi, lo], axis=1), preferred_element_type=F32)
            block = term if block is None else block + term
        rsend_ref[...] = (block[:, :128] + block[:, 128:]).reshape(groups, half, 128)

        def start_back(j, carry):
            back(j).start()
            return carry

        lax.fori_loop(1, groups, start_back, 0)
        rrecv_ref[me] = rsend_ref[me]

    for step in range(ITERS):
        v_ref[...] = jnp.dot(low_ref[...], db_ref[...], preferred_element_type=F32)
        for at in range(0, LP, CH):
            low_terms(at)
        h_ref[...] = jnp.dot(high_ref[...], wb_ref[...], preferred_element_type=F32)
        factors = None
        if step + 1 < ITERS:
            rho_new = 1.0 / (2.0 * sigma - rho)
            factors = (rho_new * rho, 2.0 * rho_new / delta)
            rho = rho_new
        squares = jnp.zeros((CH, lanes), F32)
        for at in range(0, LP, CH):
            squares = squares + finish(at, *low_result(at), factors)
        for at in range(0, HP, CH):
            squares = squares + finish(LP + at, *high_result(at), factors)
        part = jnp.sum(squares, axis=0, keepdims=True) * own_f
        folded = part[:, 0:128]
        for extra in range(1, lanes // 128):
            folded = folded + part[:, extra * 128:(extra + 1) * 128]
        part_ref[step:step + 1, :] = folded
        if step + 2 == ITERS:
            send_back()

    def norm_copy(j, slot):
        c = lax.rem(me + j, groups)
        return pltpu.make_async_remote_copy(
            src_ref=part_ref, dst_ref=nbuf_ref.at[c if slot else me], send_sem=n_send.at[j],
            recv_sem=n_recv.at[c if slot else me], device_id=(sp, c), device_id_type=mesh_id)

    def z_copy(j, slot):
        z = lax.rem(sp + j, tiles)
        return pltpu.make_async_remote_copy(
            src_ref=zpart_ref, dst_ref=zbuf_ref.at[z if slot else sp], send_sem=z_send.at[j],
            recv_sem=z_recv.at[z if slot else sp], device_id=(z, me), device_id_type=mesh_id)

    def n_start(j, carry):
        norm_copy(j, False).start()
        return carry

    def n_wait(j, carry):
        norm_copy(j, False).wait_send()
        norm_copy(j, True).wait_recv()
        return carry

    def z_start(j, carry):
        z_copy(j, False).start()
        return carry

    def z_wait(j, carry):
        z_copy(j, False).wait_send()
        z_copy(j, True).wait_recv()
        return carry

    def back_wait(j, carry):
        back(j).wait_send()
        back_in(j).wait_recv()
        return carry

    lax.fori_loop(1, groups, n_start, 0)
    nbuf_ref[me] = part_ref[...]
    lax.fori_loop(1, groups, n_wait, 0)
    zpart_ref[...] = jnp.sum(nbuf_ref[...], axis=0)
    lax.fori_loop(1, tiles, z_start, 0)
    zbuf_ref[sp] = zpart_ref[...]

    lax.fori_loop(1, groups, back_wait, 0)
    piece = rows * width
    lane_h = lax.broadcasted_iota(jnp.int32, (half, 128), 1)
    for h in range(2):
        count = min(half, cap - h * half)
        for r in range(rows):
            block = jnp.zeros((half, 128), F32)
            for c in range(groups):
                rolled = pltpu.roll(rrecv_ref[c], (c * width - h * piece - r * width) % 128, 1)
                block = jnp.where((lane_h >= c * width) & (lane_h < (c + 1) * width), rolled, block)
            out_ref[h * half:h * half + count, r, :] = block[0:count]

    lax.fori_loop(1, tiles, z_wait, 0)
    total = jnp.sum(jnp.sum(zbuf_ref[...], axis=0), axis=1, keepdims=True)
    norms_ref[...] = jnp.broadcast_to(jnp.sqrt(total), norms_ref.shape)


def local(groups, tiles, forcing, mean_field, modes, lengths):
    cap, rows, cols = forcing.shape
    width = cols // groups
    stride = width + 2 * SIDE
    lanes = round_up((rows + 2 * HALO) * stride, 128)
    capp = round_up(cap, 8)
    half = round_up(-(-cap // 2), 16)
    low, high, scales = tables()
    vmem = pl.BlockSpec(memory_space=pltpu.VMEM)
    hbm = pl.BlockSpec(memory_space=pltpu.HBM)
    dma = pltpu.SemaphoreType.DMA
    out, norms = pl.pallas_call(
        functools.partial(kernel, groups, tiles, cap, rows, cols),
        out_shape=(jax.ShapeDtypeStruct((cap, rows, cols), F32), jax.ShapeDtypeStruct((8, 128), F32)),
        in_specs=[pl.BlockSpec(memory_space=pltpu.SMEM)] + [hbm] * 6,
        out_specs=(vmem, vmem),
        scratch_shapes=[
            pltpu.VMEM((M * LP, NP), BF16), pltpu.VMEM((HP, M * LP), BF16),
            pltpu.VMEM((2, NP, 128), F32), pltpu.VMEM((cap, rows, cols), F32),
            pltpu.VMEM((groups, capp, 128), F32), pltpu.VMEM((groups, capp, 128), F32),
            pltpu.VMEM((NP, 128), F32), *[pltpu.VMEM((NP // 2, 128), F32) for _ in range(4)],
            pltpu.VMEM((3, M + 1, rows, cols), F32), pltpu.VMEM((4, M + 1, lanes), F32), pltpu.VMEM((1, lanes), F32),
            pltpu.VMEM((NP, groups * capp), BF16), pltpu.VMEM((2, groups * half, NP), BF16),
            pltpu.VMEM((NP, lanes), F32), pltpu.VMEM((NP, lanes), F32), pltpu.VMEM((NP, lanes), F32),
            pltpu.VMEM((NP, 2 * lanes), BF16), pltpu.VMEM((M * LP, 2 * lanes), F32), pltpu.VMEM((HP, 2 * lanes), F32),
            pltpu.VMEM((M * LP, 2 * lanes), BF16),
            pltpu.VMEM((groups, half, 128), F32), pltpu.VMEM((groups, half, 128), F32),
            pltpu.VMEM((8, 128), F32), pltpu.VMEM((groups, 8, 128), F32),
            pltpu.VMEM((8, 128), F32), pltpu.VMEM((tiles, 8, 128), F32),
            dma((6,)), dma((2,)), dma((2,)), dma((2,)), dma((2,)),
            dma((groups,)), dma((groups,)), dma((groups,)), dma((groups,)),
            dma((groups,)), dma((groups,)), dma((tiles,)), dma((tiles,)),
        ],
        compiler_params=pltpu.CompilerParams(collective_id=0, has_side_effects=True, vmem_limit_bytes=60 * 2**20),
        name="chebyshev",
    )(lengths, forcing, mean_field, modes, jnp.asarray(low, BF16), jnp.asarray(high, BF16), jnp.asarray(scales))
    return out, norms[:ITERS, 0]


def solution(mesh):
    in_specs = (P("chaos", "space", None), P("space", None), P(None, "space", None), P())
    out_specs = (P("chaos", "space", None), P())
    body = functools.partial(local, mesh.shape["chaos"], mesh.shape["space"])
    return jax.shard_map(body, mesh=mesh, in_specs=in_specs, out_specs=out_specs, check_vma=False)
```

```python
import functools
import math

import jax
import jax.numpy as jnp
import numpy as np
from jax import lax
from jax.experimental import pallas as pl
from jax.experimental.pallas import tpu as pltpu
from jax.sharding import PartitionSpec as P

M = 12
P_SIZE = 455
ITERS = 3
LOW = 91
LP = 96
HP = 368
NP = LP + HP
HALO = 3
SIDE = 4

spectrum_low = 0.05
spectrum_high = 3.0
F32 = jnp.float32
BF16 = jnp.bfloat16


def place(p):
    return p if p < LOW else p + (LP - LOW)


def tables():
    indices = [()]
    indices += [(a,) for a in range(M)]
    indices += [(a, b) for a in range(M) for b in range(a, M)]
    indices += [(a, b, c) for a in range(M) for b in range(a, M) for c in range(b, M)]
    lookup = {entry: number for number, entry in enumerate(indices)}
    to_low = np.zeros((M * LP, NP), np.float32)
    to_high = np.zeros((HP, M * LP), np.float32)
    scale = np.ones((NP,), np.float64)
    for number, entry in enumerate(indices):
        scale[place(number)] = math.sqrt(math.prod(math.factorial(entry.count(k)) for k in set(entry)))
        if len(entry) == 3:
            continue
        for k in range(M):
            other = lookup[tuple(sorted(entry + (k,)))]
            to_low[k * LP + number, place(other)] = entry.count(k) + 1
            if other < LOW:
                to_low[k * LP + other, place(number)] = 1.0
            else:
                to_high[place(other) - LP, k * LP + number] = 1.0
    scales = np.stack([1.0 / scale, scale]).astype(np.float32)
    scales = np.ascontiguousarray(np.broadcast_to(scales[:, :, None], (2, NP, 128)))
    return to_low, to_high, scales


def round_up(value, unit):
    return -(-value // unit) * unit


def halves(x):
    hi = x.astype(BF16)
    return hi, (x - hi.astype(F32)).astype(BF16)


def kernel(groups, tiles, cap, rows, cols, lengths_ref, forcing_hbm, mean_hbm, modes_hbm, low_hbm, high_hbm, scale_hbm,
           out_ref, norms_ref,
           low_ref, high_ref, scale_ref, forcing_ref, send_ref, recv_ref, own_ref, to_up_ref, to_down_ref, up_ref, down_ref, field_ref, coef_ref, dinv_ref,
           hot_ref, back_ref, d_ref, r_ref, s_ref, db_ref, v_ref, h_ref, wb_ref, rsend_ref, rrecv_ref, part_ref, nbuf_ref, zpart_ref, zbuf_ref,
           load_sem, f_send, f_recv, h_send, h_recv, a_send, a_recv, b_send, b_recv, n_send, n_recv, z_send, z_recv):
    me = lax.axis_index("chaos")
    sp = lax.axis_index("space")
    width = cols // groups
    stride = width + 2 * SIDE
    lanes = d_ref.shape[1]
    capp = recv_ref.shape[1]
    half = rsend_ref.shape[1]
    nx = rows * tiles
    total_rows = rows + 2 * HALO
    mesh_id = pl.DeviceIdType.MESH

    loads = [pltpu.make_async_copy(src, dst, load_sem.at[n]) for n, (src, dst) in enumerate((
        (forcing_hbm, forcing_ref), (mean_hbm, field_ref.at[1, 0]), (modes_hbm, field_ref.at[1, 1:]),
        (scale_hbm, scale_ref), (low_hbm, low_ref), (high_hbm, high_ref)))]
    for load in loads:
        load.start()

    barrier = pltpu.get_barrier_semaphore()

    def greet_group(j, carry):
        pl.semaphore_signal(barrier, inc=1, device_id=(sp, lax.rem(me + j, groups)), device_id_type=mesh_id)
        return carry

    def greet_column(j, carry):
        pl.semaphore_signal(barrier, inc=1, device_id=(lax.rem(sp + j, tiles), me), device_id_type=mesh_id)
        return carry

    lax.fori_loop(1, groups, greet_group, 0)
    lax.fori_loop(1, tiles, greet_column, 0)

    lane128 = lax.broadcasted_iota(jnp.int32, (cap, 128), 1)

    def pack(j, carry):
        c = lax.rem(me + j, groups)
        base = c * width - SIDE
        block = jnp.zeros((cap, 128), F32)
        for r in range(rows):
            shift = lax.rem(r * stride - base + 256, 128)
            rolled = pltpu.roll(forcing_ref[:, r, :], shift, 1)
            block = jnp.where((lane128 >= r * stride) & (lane128 < (r + 1) * stride), rolled, block)
        send_ref[j, 0:cap, :] = block
        if capp > cap:
            send_ref[j, cap:capp, :] = jnp.zeros((capp - cap, 128), F32)
        return carry

    def a2a(j):
        c = lax.rem(me + j, groups)
        return pltpu.make_async_remote_copy(
            src_ref=send_ref.at[j], dst_ref=recv_ref.at[me], send_sem=a_send.at[j], recv_sem=a_recv.at[me],
            device_id=(sp, c), device_id_type=mesh_id)

    def a2a_in(j):
        c = lax.rem(me + j, groups)
        return pltpu.make_async_remote_copy(
            src_ref=send_ref.at[j], dst_ref=recv_ref.at[c], send_sem=a_send.at[j], recv_sem=a_recv.at[c],
            device_id=(sp, c), device_id_type=mesh_id)

    def start_a2a(j, carry):
        a2a(j).start()
        return carry

    def pack_and_start(j, carry):
        pack(j, carry)
        a2a(j).start()
        return carry

    early = min(4, groups)
    loads[0].wait()
    for j in range(early):
        pack(j, 0)
    pl.semaphore_wait(barrier, groups - 1 + tiles - 1)
    lax.fori_loop(1, early, start_a2a, 0)
    loads[1].wait()
    loads[2].wait()

    def column(src, dst, send, recv, target):
        return pltpu.make_async_remote_copy(
            src_ref=src, dst_ref=dst, send_sem=send, recv_sem=recv, device_id=(target, me), device_id_type=mesh_id)

    up_target = lax.rem(sp + tiles - 1, tiles)
    down_target = lax.rem(sp + 1, tiles)
    has_up = sp > 0
    has_down = sp < tiles - 1
    f_up = column(field_ref.at[1], field_ref.at[2], f_send.at[0], f_recv.at[1], up_target)
    f_down = column(field_ref.at[1], field_ref.at[0], f_send.at[1], f_recv.at[0], down_target)
    f_from_up = column(field_ref.at[1], field_ref.at[0], f_send.at[0], f_recv.at[0], up_target)
    f_from_down = column(field_ref.at[1], field_ref.at[2], f_send.at[1], f_recv.at[1], down_target)

    @pl.when(has_up)
    def _():
        f_up.start()

    @pl.when(has_down)
    def _():
        f_down.start()

    lax.fori_loop(early, groups, pack_and_start, 0, unroll=groups <= 8)
    recv_ref[me] = send_ref[0]

    slots = groups * capp
    slot = lax.broadcasted_iota(jnp.int32, (1, slots), 1)
    coef = jnp.full((1, slots), -1, jnp.int32)
    start = jnp.int32(0)
    starts = []
    for g in range(groups):
        count = lengths_ref[g]
        here = slot - g * capp
        coef = jnp.where((here >= 0) & (here < count), start + here, coef)
        starts.append(start)
        start = start + count
    row = lax.broadcasted_iota(jnp.int32, (NP, slots), 0)
    row_coef = jnp.where(row < LOW, row, jnp.where(row < LP, -2, row - (LP - LOW)))
    hot_ref[...] = jnp.where(row_coef == coef, 1.0, 0.0).astype(BF16)
    p_lane = lax.broadcasted_iota(jnp.int32, (half, NP), 1)
    p_coef = jnp.where(p_lane < LOW, p_lane, jnp.where(p_lane < LP, -2, p_lane - (LP - LOW)))
    t = lax.broadcasted_iota(jnp.int32, (half, NP), 0)
    for h in range(2):
        tt = t + h * half
        for g in range(groups):
            hot = jnp.where((tt < lengths_ref[g]) & (p_coef - tt == starts[g]), 1.0, 0.0).astype(BF16)
            back_ref[h, g * half:(g + 1) * half, :] = hot

    @pl.when(jnp.logical_not(has_up))
    def _():
        field_ref[0] = jnp.zeros(field_ref.shape[1:], F32)
        up_ref[...] = jnp.zeros(up_ref.shape, F32)

    @pl.when(jnp.logical_not(has_down))
    def _():
        field_ref[2] = jnp.zeros(field_ref.shape[1:], F32)
        down_ref[...] = jnp.zeros(down_ref.shape, F32)

    @pl.when(has_up)
    def _():
        f_up.wait_send()
        f_from_up.wait_recv()

    @pl.when(has_down)
    def _():
        f_down.wait_send()
        f_from_down.wait_recv()

    base = me * width - SIDE
    n_fields = M + 1
    lane_f = lax.broadcasted_iota(jnp.int32, (n_fields, lanes), 1)
    col_f = lax.broadcasted_iota(jnp.int32, (n_fields, cols), 1)
    first_field = lax.broadcasted_iota(jnp.int32, (n_fields, cols), 0) == 0

    def field_row(g):
        x = field_ref[g // rows, :, g % rows, :]
        return jnp.where(first_field, x, x * x[0:1, :])

    skip = rows - HALO - 1
    fields = [field_row(skip + g) for g in range(total_rows + 2)]
    packed = [jnp.zeros((n_fields, lanes), F32) for _ in range(4)]
    valid = jnp.zeros((1, lanes), jnp.bool_)
    lane1 = lax.broadcasted_iota(jnp.int32, (1, lanes), 1)
    for r in range(total_rows):
        here = fields[r + 1]
        east = jnp.where(col_f < cols - 1, pltpu.roll(here, cols - 1, 1), 0.0)
        west = jnp.where(col_f > 0, pltpu.roll(here, 1, 1), 0.0)
        shift = lax.rem(r * stride - base + 512, 128)
        at = lane1 - r * stride
        inside = ((at >= 0) & (at < stride) & (at + base >= 0) & (at + base < cols)
                  & (sp * rows - HALO + r >= 0) & (sp * rows - HALO + r < nx))
        valid = valid | inside
        for n, other in enumerate((east, west, fields[r + 2], fields[r])):
            rolled = pltpu.roll(0.5 * (here + other), shift, 1)
            if lanes > 128:
                rolled = jnp.concatenate([rolled] * (lanes // 128), axis=1)
            packed[n] = jnp.where(inside, rolled, packed[n])
    for n in range(4):
        coef_ref[n] = packed[n]
    diagonal = packed[0][0:1] + packed[1][0:1] + packed[2][0:1] + packed[3][0:1]
    dinv_ref[...] = jnp.where(valid, 1.0 / jnp.where(valid, diagonal, 1.0), 0.0)

    def wait_a2a(j, carry):
        a2a(j).wait_send()
        a2a_in(j).wait_recv()
        return carry

    lax.fori_loop(1, groups, wait_a2a, 0)
    hi, lo = halves(recv_ref[...].reshape(slots, 128))
    both = jnp.dot(hot_ref[...], jnp.concatenate([hi, lo], axis=1), preferred_element_type=F32)
    loads[3].wait()
    own = (both[:, :128] + both[:, 128:]) * scale_ref[0]
    own_ref[...] = own

    np2 = NP // 2
    lane_2 = lax.broadcasted_iota(jnp.int32, (np2, 128), 1)
    segments = []
    offset = 0
    for e in range(1, HALO + 1):
        segments.append((e, offset, width + 2 * (HALO - e), SIDE - (HALO - e)))
        offset += width + 2 * (HALO - e)

    def pack_halo(row_at):
        block = jnp.zeros((np2, 128), F32)
        for part in range(2):
            source = own[part * np2:(part + 1) * np2]
            for e, offset, size, column_at in segments:
                target = part * 64 + offset
                rolled = pltpu.roll(source, (target - row_at(e) * stride - column_at) % 128, 1)
                block = jnp.where((lane_2 >= target) & (lane_2 < target + size), rolled, block)
        return block

    to_up_ref[...] = pack_halo(lambda e: e - 1)
    to_down_ref[...] = pack_halo(lambda e: rows - e)

    h_up = column(to_up_ref, down_ref, h_send.at[0], h_recv.at[1], up_target)
    h_down = column(to_down_ref, up_ref, h_send.at[1], h_recv.at[0], down_target)
    h_from_up = column(to_down_ref, up_ref, h_send.at[0], h_recv.at[0], up_target)
    h_from_down = column(to_up_ref, down_ref, h_send.at[1], h_recv.at[1], down_target)

    @pl.when(has_up)
    def _():
        h_up.start()

    @pl.when(has_down)
    def _():
        h_down.start()

    @pl.when(has_up)
    def _():
        h_up.wait_send()
        h_from_up.wait_recv()

    @pl.when(has_down)
    def _():
        h_down.wait_send()
        h_from_down.wait_recv()

    lane_n = lax.broadcasted_iota(jnp.int32, (NP, 128), 1)

    lane_w = lax.broadcasted_iota(jnp.int32, (np2, lanes), 1)

    def wide(block, shift):
        block = pltpu.roll(block, shift % 128, 1)
        return jnp.concatenate([block] * (lanes // 128), axis=1) if lanes > 128 else block

    def assemble(part):
        mine = wide(own_ref[part * np2:(part + 1) * np2, :], HALO * stride)
        block = jnp.where((lane_w >= HALO * stride) & (lane_w < (HALO + rows) * stride), mine, 0.0)
        for source, row_at in ((up_ref[...], lambda e: HALO - e), (down_ref[...], lambda e: HALO + rows - 1 + e)):
            for e, offset, size, column_at in segments:
                target = row_at(e) * stride + column_at
                moved = wide(source, target - part * 64 - offset)
                block = jnp.where((lane_w >= target) & (lane_w < target + size), moved, block)
        return block

    theta = (spectrum_high + spectrum_low) / 2.0
    delta = (spectrum_high - spectrum_low) / 2.0
    sigma = theta / delta
    rho = 1.0 / sigma
    for part in range(2):
        here = slice(part * np2, (part + 1) * np2)
        first = assemble(part)
        r_ref[here, :] = first
        first = first * (dinv_ref[...] * (1.0 / theta))
        d_ref[here, :] = first
        s_ref[here, :] = first
        hi, lo = halves(first)
        db_ref[here, 0:lanes] = hi
        db_ref[here, lanes:] = lo

    own_lane = jnp.zeros((1, lanes), jnp.bool_)
    for r in range(rows):
        at = lane1 - (HALO + r) * stride - SIDE
        own_lane = own_lane | ((at >= 0) & (at < width))
    own_f = jnp.where(own_lane, 1.0, 0.0)

    loads[4].wait()
    loads[5].wait()
    part_ref[...] = jnp.zeros(part_ref.shape, F32)

    def neighbours(x):
        return (pltpu.roll(x, lanes - 1, 1), pltpu.roll(x, 1, 1),
                pltpu.roll(x, lanes - stride, 1), pltpu.roll(x, stride, 1))

    CH = 16

    def low_terms(at):
        x = d_ref[at:at + CH, :]
        diffs = [x - y for y in neighbours(x)]
        for k in range(M):
            w = coef_ref[0, k + 1:k + 2, :] * diffs[0]
            for n in range(1, 4):
                w = w + coef_ref[n, k + 1:k + 2, :] * diffs[n]
            hi, lo = halves(w)
            wb_ref[k * LP + at:k * LP + at + CH, 0:lanes] = hi
            wb_ref[k * LP + at:k * LP + at + CH, lanes:] = lo

    def low_result(at):
        x = d_ref[at:at + CH, :]
        sums = [coef_ref[n, 0:1, :] * x for n in range(4)]
        for k in range(M):
            there = k * LP + at
            v = v_ref[there:there + CH, 0:lanes] + v_ref[there:there + CH, lanes:]
            for n in range(4):
                sums[n] = sums[n] + coef_ref[n, k + 1:k + 2, :] * v
        result = (sums[0] + sums[1]) + (sums[2] + sums[3])
        result = result - pltpu.roll(sums[0], 1, 1) - pltpu.roll(sums[1], lanes - 1, 1)
        return x, result - pltpu.roll(sums[2], stride, 1) - pltpu.roll(sums[3], lanes - stride, 1)

    def high_result(at):
        x = d_ref[LP + at:LP + at + CH, :]
        result = h_ref[at:at + CH, 0:lanes] + h_ref[at:at + CH, lanes:]
        for n, y in enumerate(neighbours(x)):
            result = result + coef_ref[n, 0:1, :] * (x - y)
        return x, result

    def finish(at, x, result, factors):
        residual = r_ref[at:at + CH, :] - result
        scale = scale_ref[1, at:at + CH, :]
        if lanes > 128:
            scale = jnp.concatenate([scale] * (lanes // 128), axis=1)
        scaled = residual * scale
        if factors is not None:
            r_ref[at:at + CH, :] = residual
            new = factors[0] * x + factors[1] * (residual * dinv_ref[...])
            d_ref[at:at + CH, :] = new
            s_ref[at:at + CH, :] = s_ref[at:at + CH, :] + new
            hi, lo = halves(new)
            db_ref[at:at + CH, 0:lanes] = hi
            db_ref[at:at + CH, lanes:] = lo
        return scaled * scaled

    def back(j):
        c = lax.rem(me + j, groups)
        return pltpu.make_async_remote_copy(
            src_ref=rsend_ref.at[c], dst_ref=rrecv_ref.at[me], send_sem=b_send.at[j], recv_sem=b_recv.at[me],
            device_id=(sp, c), device_id_type=mesh_id)

    def back_in(j):
        c = lax.rem(me + j, groups)
        return pltpu.make_async_remote_copy(
            src_ref=rsend_ref.at[c], dst_ref=rrecv_ref.at[c], send_sem=b_send.at[j], recv_sem=b_recv.at[c],
            device_id=(sp, c), device_id_type=mesh_id)

    def send_back():
        piece = rows * width
        s = s_ref[...]
        q1 = jnp.zeros((NP, 128), F32)
        q2 = jnp.zeros((NP, 128), F32)
        for r in range(rows):
            origin = (HALO + r) * stride + SIDE
            a = pltpu.roll(s, (r * width - origin) % lanes, 1)[:, :128]
            b = pltpu.roll(s, (piece + r * width - origin) % lanes, 1)[:, :128]
            q1 = jnp.where((lane_n >= r * width) & (lane_n < (r + 1) * width), a, q1)
            q2 = jnp.where((lane_n >= piece + r * width) & (lane_n < piece + (r + 1) * width), b, q2)
        block = None
        for h, q in enumerate((q1, q2)):
            hi, lo = halves(q * scale_ref[1])
            term = jnp.dot(back_ref[h], jnp.concatenate([hi, lo], axis=1), preferred_element_type=F32)
            block = term if block is None else block + term
        rsend_ref[...] = (block[:, :128] + block[:, 128:]).reshape(groups, half, 128)

        def start_back(j, carry):
            back(j).start()
            return carry

        lax.fori_loop(1, groups, start_back, 0)
        rrecv_ref[me] = rsend_ref[me]

    for step in range(ITERS):
        v_ref[...] = jnp.dot(low_ref[...], db_ref[...], preferred_element_type=F32)
        for at in range(0, LP, CH):
            low_terms(at)
        h_ref[...] = jnp.dot(high_ref[...], wb_ref[...], preferred_element_type=F32)
        factors = None
        if step + 1 < ITERS:
            rho_new = 1.0 / (2.0 * sigma - rho)
            factors = (rho_new * rho, 2.0 * rho_new / delta)
            rho = rho_new
        squares = jnp.zeros((CH, lanes), F32)
        for at in range(0, LP, CH):
            squares = squares + finish(at, *low_result(at), factors)
        for at in range(0, HP, CH):
            squares = squares + finish(LP + at, *high_result(at), factors)
        part = jnp.sum(squares, axis=0, keepdims=True) * own_f
        folded = part[:, 0:128]
        for extra in range(1, lanes // 128):
            folded = folded + part[:, extra * 128:(extra + 1) * 128]
        part_ref[step:step + 1, :] = folded
        if step + 2 == ITERS:
            send_back()

    def norm_copy(j, slot):
        c = lax.rem(me + j, groups)
        return pltpu.make_async_remote_copy(
            src_ref=part_ref, dst_ref=nbuf_ref.at[c if slot else me], send_sem=n_send.at[j],
            recv_sem=n_recv.at[c if slot else me], device_id=(sp, c), device_id_type=mesh_id)

    def z_copy(j, slot):
        z = lax.rem(sp + j, tiles)
        return pltpu.make_async_remote_copy(
            src_ref=zpart_ref, dst_ref=zbuf_ref.at[z if slot else sp], send_sem=z_send.at[j],
            recv_sem=z_recv.at[z if slot else sp], device_id=(z, me), device_id_type=mesh_id)

    def n_start(j, carry):
        norm_copy(j, False).start()
        return carry

    def n_wait(j, carry):
        norm_copy(j, False).wait_send()
        norm_copy(j, True).wait_recv()
        return carry

    def z_start(j, carry):
        z_copy(j, False).start()
        return carry

    def z_wait(j, carry):
        z_copy(j, False).wait_send()
        z_copy(j, True).wait_recv()
        return carry

    def back_wait(j, carry):
        back(j).wait_send()
        back_in(j).wait_recv()
        return carry

    piece = rows * width
    lane_h = lax.broadcasted_iota(jnp.int32, (half, 128), 1)

    def unpack(h):
        count = min(half, cap - h * half)
        for r in range(rows):
            block = jnp.zeros((half, 128), F32)
            for c in range(groups):
                rolled = pltpu.roll(rrecv_ref[c], (c * width - h * piece - r * width) % 128, 1)
                block = jnp.where((lane_h >= c * width) & (lane_h < (c + 1) * width), rolled, block)
            out_ref[h * half:h * half + count, r, :] = block[0:count]

    lax.fori_loop(1, groups, n_start, 0)
    nbuf_ref[me] = part_ref[...]
    lax.fori_loop(1, groups, back_wait, 0)
    unpack(0)
    lax.fori_loop(1, groups, n_wait, 0)
    zpart_ref[...] = jnp.sum(nbuf_ref[...], axis=0)
    lax.fori_loop(1, tiles, z_start, 0)
    zbuf_ref[sp] = zpart_ref[...]
    unpack(1)
    lax.fori_loop(1, tiles, z_wait, 0)
    total = jnp.sum(jnp.sum(zbuf_ref[...], axis=0), axis=1, keepdims=True)
    norms_ref[...] = jnp.broadcast_to(jnp.sqrt(total), norms_ref.shape)


def local(groups, tiles, forcing, mean_field, modes, lengths):
    cap, rows, cols = forcing.shape
    width = cols // groups
    stride = width + 2 * SIDE
    lanes = round_up((rows + 2 * HALO) * stride, 128)
    capp = round_up(cap, 8)
    half = round_up(-(-cap // 2), 16)
    low, high, scales = tables()
    vmem = pl.BlockSpec(memory_space=pltpu.VMEM)
    hbm = pl.BlockSpec(memory_space=pltpu.HBM)
    dma = pltpu.SemaphoreType.DMA
    out, norms = pl.pallas_call(
        functools.partial(kernel, groups, tiles, cap, rows, cols),
        out_shape=(jax.ShapeDtypeStruct((cap, rows, cols), F32), jax.ShapeDtypeStruct((8, 128), F32)),
        in_specs=[pl.BlockSpec(memory_space=pltpu.SMEM)] + [hbm] * 6,
        out_specs=(vmem, vmem),
        scratch_shapes=[
            pltpu.VMEM((M * LP, NP), BF16), pltpu.VMEM((HP, M * LP), BF16),
            pltpu.VMEM((2, NP, 128), F32), pltpu.VMEM((cap, rows, cols), F32),
            pltpu.VMEM((groups, capp, 128), F32), pltpu.VMEM((groups, capp, 128), F32),
            pltpu.VMEM((NP, 128), F32), *[pltpu.VMEM((NP // 2, 128), F32) for _ in range(4)],
            pltpu.VMEM((3, M + 1, rows, cols), F32), pltpu.VMEM((4, M + 1, lanes), F32), pltpu.VMEM((1, lanes), F32),
            pltpu.VMEM((NP, groups * capp), BF16), pltpu.VMEM((2, groups * half, NP), BF16),
            pltpu.VMEM((NP, lanes), F32), pltpu.VMEM((NP, lanes), F32), pltpu.VMEM((NP, lanes), F32),
            pltpu.VMEM((NP, 2 * lanes), BF16), pltpu.VMEM((M * LP, 2 * lanes), F32), pltpu.VMEM((HP, 2 * lanes), F32),
            pltpu.VMEM((M * LP, 2 * lanes), BF16),
            pltpu.VMEM((groups, half, 128), F32), pltpu.VMEM((groups, half, 128), F32),
            pltpu.VMEM((8, 128), F32), pltpu.VMEM((groups, 8, 128), F32),
            pltpu.VMEM((8, 128), F32), pltpu.VMEM((tiles, 8, 128), F32),
            dma((6,)), dma((2,)), dma((2,)), dma((2,)), dma((2,)),
            dma((groups,)), dma((groups,)), dma((groups,)), dma((groups,)),
            dma((groups,)), dma((groups,)), dma((tiles,)), dma((tiles,)),
        ],
        compiler_params=pltpu.CompilerParams(collective_id=0, has_side_effects=True, vmem_limit_bytes=60 * 2**20),
        name="chebyshev",
    )(lengths, forcing, mean_field, modes, jnp.asarray(low, BF16), jnp.asarray(high, BF16), jnp.asarray(scales))
    return out, norms[:ITERS, 0]


def solution(mesh):
    in_specs = (P("chaos", "space", None), P("space", None), P(None, "space", None), P())
    out_specs = (P("chaos", "space", None), P())
    body = functools.partial(local, mesh.shape["chaos"], mesh.shape["space"])
    return jax.shard_map(body, mesh=mesh, in_specs=in_specs, out_specs=out_specs, check_vma=False)
```
